32 devices in a mesh: ctx: 8 (over z, core), comp: 4 (over y, x).
Axes of the slice: x: 2, y: 2, z: 4, core: 2. Of those that a mesh axis runs over, the one named last changes fastest.
Arguments:
- prompt_query: bfloat16 [4, 1024, 4096], P('comp', 'ctx'), may hold values from -6 to 6
- prompt_kv: bfloat16 [4, 1024, 1024], P('comp', 'ctx'), may hold values from -6 to 6
- prompt_cot: bfloat16 [4, 1024, 4096], P('comp', 'ctx'), may hold values from -6 to 6
- comp_query: bfloat16 [32, 128, 4096], P(('ctx', 'comp')), may hold values from -6 to 6
- comp_kv: bfloat16 [32, 128, 1024], P(('ctx', 'comp')), may hold values from -6 to 6
- comp_cot: bfloat16 [32, 128, 4096], P(('ctx', 'comp')), may hold values from -6 to 6
- group_of: int32 [32], replicated, may hold values from 0 to 3, as said below
- lengths: int32 [32], replicated, may hold values from 32 to 128
Outputs:
- prompt_dq: bfloat16 [4, 1024, 4096], P('comp', 'ctx')
- prompt_dkv: bfloat16 [4, 1024, 1024], P('comp', 'ctx')
- comp_dq: bfloat16 [32, 128, 4096], P(('ctx', 'comp'))
- comp_dkv: bfloat16 [32, 128, 1024], P(('ctx', 'comp'))
The draws below stay inside these ranges and needn't reach their ends.
Inputs may be any that keep to these rules, and one draw needn't show every extreme that they name: `group_of`: each group number is named by exactly 8 completions.
All inputs are finite; a program needn't handle non-finite values.
Results may differ from the reference program's by a relative error of at most 0.023.
Values may be sent and summed in bfloat16 or wider, within the bound.
A program may use at most 128 MiB of HBM per device.

```python
import math
import jax
import jax.numpy as jnp
from jax import lax

QUERY_HEADS = 32
KEY_VALUE_HEADS = 4
HEAD_SIZE = 128
COMPLETION_SLOTS = 128
PROMPT_TOKENS = 1024
GROUP_TOTAL = 4
COMPLETION_TOTAL = 32


def draw_prompt_kv(key, part):
    key = jax.random.fold_in(key, 3)
    tensor_shape = (GROUP_TOTAL, PROMPT_TOKENS, 2 * KEY_VALUE_HEADS * HEAD_SIZE)
    sampled_values = jax.random.truncated_normal(key, -4.0, 4.0, tensor_shape, jnp.float32)
    return sampled_values.astype(jnp.bfloat16)


def draw_prompt_query(key, part):
    key = jax.random.fold_in(key, 5)
    tensor_shape = (GROUP_TOTAL, PROMPT_TOKENS, QUERY_HEADS * HEAD_SIZE)
    sampled_values = jax.random.truncated_normal(key, -4.0, 4.0, tensor_shape, jnp.float32)
    return sampled_values.astype(jnp.bfloat16)


def draw_comp_query(key, part):
    key = jax.random.fold_in(key, 7)
    tensor_shape = (COMPLETION_TOTAL, COMPLETION_SLOTS, QUERY_HEADS * HEAD_SIZE)
    sampled_values = jax.random.truncated_normal(key, -4.0, 4.0, tensor_shape, jnp.float32)
    return sampled_values.astype(jnp.bfloat16)


def draw_comp_kv(key, part):
    key = jax.random.fold_in(key, 11)
    tensor_shape = (COMPLETION_TOTAL, COMPLETION_SLOTS, 2 * KEY_VALUE_HEADS * HEAD_SIZE)
    sampled_values = jax.random.truncated_normal(key, -4.0, 4.0, tensor_shape, jnp.float32)
    return sampled_values.astype(jnp.bfloat16)


def draw_group_of(key, part):
    key = jax.random.fold_in(key, 13)
    labels = jnp.arange(COMPLETION_TOTAL, dtype=jnp.int32) % GROUP_TOTAL
    return jax.random.permutation(key, labels).astype(jnp.int32)


def draw_lengths(key, part):
    key = jax.random.fold_in(key, 17)
    first_key, spot_key = jax.random.split(key)
    sampled_values = jax.random.randint(first_key, (COMPLETION_TOTAL,), COMPLETION_SLOTS // 4, COMPLETION_SLOTS + 1)
    spot_index = jax.random.randint(spot_key, (), 0, COMPLETION_TOTAL)
    return sampled_values.at[spot_index].set(COMPLETION_SLOTS).astype(jnp.int32)


def steps_of(rng, extent, shards, least, top_value):
    level, own = 1.0, jax.random.fold_in(rng, 6)
    for axis_at, parts in shards:
        draws = jnp.exp(jax.random.uniform(jax.random.fold_in(own, axis_at), (parts,), jnp.float32, least / len(shards), top_value / len(shards)))
        level = level * jnp.repeat(draws, extent[axis_at] // parts).reshape([-1 if axis == axis_at else 1 for axis in range(len(extent))])
    return level


def noise(stream_key, dims, spread, bound, cuts=(), kind=jnp.bfloat16):
    values = spread * jax.random.normal(stream_key, dims, jnp.float32)
    if cuts:
        values = values * steps_of(stream_key, dims, cuts, -0.22, 0.18)
    return jnp.clip(values, -bound, bound).astype(kind)


def setup_inputs(seed: int = 0) -> dict:
    arg_keys = jax.random.split(jax.random.key(seed), 9)
    return {
        "prompt_query": draw_prompt_query(jax.random.fold_in(arg_keys[8], 71), 0),
        "prompt_kv": draw_prompt_kv(jax.random.fold_in(arg_keys[8], 71), 0),
        "prompt_cot": noise(arg_keys[2], (GROUP_TOTAL, PROMPT_TOKENS, QUERY_HEADS * HEAD_SIZE), 1.0, 6.0, ((0, 4), (1, 8))),
        "comp_query": draw_comp_query(jax.random.fold_in(arg_keys[8], 71), 0),
        "comp_kv": draw_comp_kv(jax.random.fold_in(arg_keys[8], 71), 0),
        "comp_cot": noise(arg_keys[5], (COMPLETION_TOTAL, COMPLETION_SLOTS, QUERY_HEADS * HEAD_SIZE), 1.0, 6.0, ((0, 32),)),
        "group_of": draw_group_of(jax.random.fold_in(arg_keys[8], 71), 0),
        "lengths": draw_lengths(jax.random.fold_in(arg_keys[8], 71), 0),
    }


MASK_FILL = -1e+30

def rounded(values):
    return lax.optimization_barrier(values.astype(jnp.bfloat16)).astype(jnp.float32)

def dense_attention(query_rows, output_cotangent, key_tensor, allowed):
    row_total = query_rows.shape[0]
    key_total = key_tensor.shape[0]
    query_per_key_head = QUERY_HEADS // KEY_VALUE_HEADS
    scaling = 1.0 / math.sqrt(HEAD_SIZE)
    half_extent = KEY_VALUE_HEADS * HEAD_SIZE
    query_by_head = query_rows.astype(jnp.float32).reshape(row_total, KEY_VALUE_HEADS, query_per_key_head, HEAD_SIZE)
    cotangent_by_head = output_cotangent.astype(jnp.float32).reshape(row_total, KEY_VALUE_HEADS, query_per_key_head, HEAD_SIZE)
    key_row_list = key_tensor[:, :half_extent].astype(jnp.float32).reshape(key_total, KEY_VALUE_HEADS, HEAD_SIZE)
    value_row_list = key_tensor[:, half_extent:].astype(jnp.float32).reshape(key_total, KEY_VALUE_HEADS, HEAD_SIZE)
    scores = jnp.einsum('rhgd,khd->hgrk', query_by_head, key_row_list) * scaling
    scores = jnp.where(allowed[None, None], scores, MASK_FILL)
    row_max = lax.optimization_barrier(jnp.max(scores, axis=-1))
    row_sum = lax.optimization_barrier(jnp.sum(jnp.exp(scores - row_max[..., None]), axis=-1))
    weights = rounded(jnp.exp(scores - row_max[..., None]))
    output = jnp.einsum('hgrk,khd->hgrd', weights, value_row_list) / row_sum[..., None]
    lse = row_max + jnp.log(row_sum)
    row_delta = lax.optimization_barrier(jnp.sum(cotangent_by_head.transpose(1, 2, 0, 3) * output, axis=-1))
    probability = jnp.exp(scores - lse[..., None])
    prob_half = rounded(probability)
    value_grad = jnp.einsum('hgrk,rhgd->khd', prob_half, cotangent_by_head)
    prob_grad = jnp.einsum('rhgd,khd->hgrk', cotangent_by_head, value_row_list)
    score_grad = rounded(probability * (prob_grad - row_delta[..., None]) * scaling)
    query_gradient = jnp.einsum('hgrk,khd->rhgd', score_grad, key_row_list).reshape(row_total, -1)
    key_grad = jnp.einsum('hgrk,rhgd->khd', score_grad, query_by_head)
    key_terms = jnp.concatenate([key_grad.reshape(key_total, -1), value_grad.reshape(key_total, -1)], axis=1)
    return (query_gradient, key_terms)

def reference(prompt_query, prompt_kv, prompt_cot, comp_query, comp_kv, comp_cot, group_of, lengths):
    key_block = min(512, PROMPT_TOKENS)
    block_total = PROMPT_TOKENS // key_block
    row_extent = 2 * KEY_VALUE_HEADS * HEAD_SIZE
    key_pos = jnp.arange(PROMPT_TOKENS, dtype=jnp.int32)

    def prompt_group(inputs):
        query_rows, key_tensor, output_cotangent = inputs

        def query_block(summed, block_index):
            offset = block_index * key_block
            block_query = lax.dynamic_slice_in_dim(query_rows, offset, key_block, 0)
            block_cotangent = lax.dynamic_slice_in_dim(output_cotangent, offset, key_block, 0)
            positions = offset + jnp.arange(key_block, dtype=jnp.int32)
            allowed = positions[:, None] >= key_pos[None, :]
            query_gradient, key_terms = dense_attention(block_query, block_cotangent, key_tensor, allowed)
            return (summed + key_terms, query_gradient)
        summed, query_gradient = lax.scan(query_block, jnp.zeros((PROMPT_TOKENS, row_extent), jnp.float32), jnp.arange(block_total, dtype=jnp.int32))
        return (query_gradient.reshape(PROMPT_TOKENS, -1), summed)
    prompt_grad, prompt_terms = lax.map(prompt_group, (prompt_query, prompt_kv, prompt_cot))
    own_pos = jnp.arange(COMPLETION_SLOTS, dtype=jnp.int32)

    def completion(group_table, comp_index):
        group_id = group_of[comp_index]
        length = lengths[comp_index]
        is_valid = own_pos < length
        key_tensor = jnp.concatenate([prompt_kv[group_id], comp_kv[comp_index]], axis=0)
        own_allowed = (own_pos[None, :] <= own_pos[:, None]) & is_valid[None, :]
        allowed = jnp.concatenate([jnp.ones((COMPLETION_SLOTS, PROMPT_TOKENS), dtype=bool), own_allowed], axis=1)
        output_cotangent = jnp.where(is_valid[:, None], comp_cot[comp_index], jnp.zeros_like(comp_cot[comp_index]))
        query_gradient, key_terms = dense_attention(comp_query[comp_index], output_cotangent, key_tensor, allowed)
        group_table = group_table.at[group_id].add(key_terms[:PROMPT_TOKENS])
        return (group_table, (query_gradient, key_terms[PROMPT_TOKENS:]))
    group_table, (comp_grad, own_terms) = lax.scan(completion, prompt_terms, jnp.arange(COMPLETION_TOTAL, dtype=jnp.int32))
    return (prompt_grad.astype(jnp.bfloat16), group_table.astype(jnp.bfloat16), comp_grad.astype(jnp.bfloat16), own_terms.astype(jnp.bfloat16))
```

```python
import functools
import math

import jax
import jax.numpy as jnp
from jax import lax
from jax.experimental import pallas as pl
from jax.experimental.pallas import tpu as pltpu
from jax.sharding import PartitionSpec as P

QUERY_HEADS = 32
KEY_VALUE_HEADS = 4
HEAD_SIZE = 128
GROUP = QUERY_HEADS // KEY_VALUE_HEADS
HALF = KEY_VALUE_HEADS * HEAD_SIZE
PAIR = 2
SCALING = 1.0 / math.sqrt(HEAD_SIZE)

MASK_FILL = -1e30


def heads_to_rows(block, first, count):
    parts = [block[:, (first + i) * HEAD_SIZE : (first + i + 1) * HEAD_SIZE] for i in range(count)]
    return jnp.concatenate(parts, axis=0)


def head_gradients(query, cotangent, keys, values, bias, prob_ref, grad_ref, dq_ref):
    exponent = SCALING * math.log2(math.e)
    rows = query.shape[0]
    for pair in range(GROUP // PAIR):
        q = heads_to_rows(query, pair * PAIR, PAIR)
        c = heads_to_rows(cotangent, pair * PAIR, PAIR)
        scores = lax.dot_general(
            keys, q, (((1,), (1,)), ((), ())), preferred_element_type=jnp.float32
        )
        scores = bias(scores)
        prob_grad = lax.dot_general(
            values, c, (((1,), (1,)), ((), ())), preferred_element_type=jnp.float32
        )
        row_max = jnp.max(scores, axis=0, keepdims=True)
        weights = jnp.exp2((scores - row_max) * exponent)
        inverse = 1.0 / jnp.sum(weights, axis=0, keepdims=True)
        delta = jnp.sum(weights * prob_grad, axis=0, keepdims=True) * inverse
        probability = weights * inverse
        score_grad = (probability * (prob_grad - delta)).astype(jnp.bfloat16)
        columns = slice(pair * PAIR * rows, (pair + 1) * PAIR * rows)
        prob_ref[:, columns] = probability.astype(jnp.bfloat16)
        grad_ref[:, columns] = score_grad
        dq = lax.dot_general(
            score_grad, keys, (((0,), (0,)), ((), ())), preferred_element_type=jnp.float32
        )
        dq = (dq * SCALING).astype(jnp.bfloat16)
        for i in range(PAIR):
            at = (pair * PAIR + i) * HEAD_SIZE
            dq_ref[:, at : at + HEAD_SIZE] = dq[i * rows : (i + 1) * rows]
    key_grad = jnp.dot(
        grad_ref[...], heads_to_rows(query, 0, GROUP), preferred_element_type=jnp.float32
    )
    value_grad = jnp.dot(
        prob_ref[...], heads_to_rows(cotangent, 0, GROUP), preferred_element_type=jnp.float32
    )
    return (key_grad * SCALING).astype(jnp.bfloat16), value_grad.astype(jnp.bfloat16)


def prompt_kernel(place_ref, q_ref, c_ref, k_ref, v_ref, dq_ref, dk_ref, dv_ref, bias_ref, prob_ref, grad_ref):
    rows = q_ref.shape[0]
    total = k_ref.shape[0]

    @pl.when(pl.program_id(0) == 0)
    def _():
        shape = (total, rows)
        key_at = lax.broadcasted_iota(jnp.int32, shape, 0)
        row_at = lax.broadcasted_iota(jnp.int32, shape, 1)
        allowed = key_at <= row_at + place_ref[0] * rows
        bias_ref[...] = jnp.where(allowed, 0.0, MASK_FILL)

    def bias(scores):
        return scores + jnp.concatenate([bias_ref[...]] * PAIR, axis=1)

    dk, dv = head_gradients(
        q_ref[...], c_ref[...], k_ref[...], v_ref[...], bias, prob_ref, grad_ref, dq_ref
    )
    dk_ref[...] = dk
    dv_ref[...] = dv


def completion_kernel(length_ref, q_ref, c_ref, k_ref, v_ref, own_k_ref, own_v_ref, dq_ref, dk_ref, dv_ref, own_dk_ref, own_dv_ref, prob_ref, grad_ref):
    rows = q_ref.shape[0]
    total = k_ref.shape[0]
    length = length_ref[0]
    key_at = lax.broadcasted_iota(jnp.int32, (rows, rows), 0)
    row_at = lax.broadcasted_iota(jnp.int32, (rows, rows), 1)
    own_bias = jnp.where((key_at <= row_at) & (key_at < length), 0.0, MASK_FILL)

    def bias(scores):
        own = scores[total:] + jnp.concatenate([own_bias] * PAIR, axis=1)
        return jnp.concatenate([scores[:total], own], axis=0)

    cotangent = c_ref[...]
    live = lax.broadcasted_iota(jnp.int32, cotangent.shape, 0) < length
    cotangent = jnp.where(live, cotangent, jnp.zeros_like(cotangent))
    keys = jnp.concatenate([k_ref[...], own_k_ref[...]], axis=0)
    values = jnp.concatenate([v_ref[...], own_v_ref[...]], axis=0)
    dk, dv = head_gradients(q_ref[...], cotangent, keys, values, bias, prob_ref, grad_ref, dq_ref)
    dk_ref[...] = dk[:total]
    dv_ref[...] = dv[:total]
    own_dk_ref[...] = dk[total:]
    own_dv_ref[...] = dv[total:]


def lane_block(rows, width, shift=0):
    return pl.BlockSpec((rows, width), lambda h, _: (0, h + shift))


def params():
    return pltpu.CompilerParams(vmem_limit_bytes=56 * 1024 * 1024)


def prompt_attention(query, cotangent, kv, place):
    rows, total = query.shape[0], kv.shape[0]
    wide = GROUP * HEAD_SIZE
    return pl.pallas_call(
        prompt_kernel,
        grid_spec=pltpu.PrefetchScalarGridSpec(
            num_scalar_prefetch=1,
            grid=(KEY_VALUE_HEADS,),
            in_specs=[
                lane_block(rows, wide),
                lane_block(rows, wide),
                lane_block(total, HEAD_SIZE),
                lane_block(total, HEAD_SIZE, KEY_VALUE_HEADS),
            ],
            out_specs=[
                lane_block(rows, wide),
                lane_block(total, HEAD_SIZE),
                lane_block(total, HEAD_SIZE),
            ],
            scratch_shapes=[
                pltpu.VMEM((total, rows), jnp.float32),
                pltpu.VMEM((total, GROUP * rows), jnp.bfloat16),
                pltpu.VMEM((total, GROUP * rows), jnp.bfloat16),
            ],
        ),
        out_shape=[
            jax.ShapeDtypeStruct(query.shape, jnp.bfloat16),
            jax.ShapeDtypeStruct((total, HALF), jnp.bfloat16),
            jax.ShapeDtypeStruct((total, HALF), jnp.bfloat16),
        ],
        compiler_params=params(),
        name="prompt_attention",
    )(place, query, cotangent, kv, kv)


def completion_attention(query, cotangent, kv, own_kv, length):
    rows, total = query.shape[0], kv.shape[0]
    wide = GROUP * HEAD_SIZE
    return pl.pallas_call(
        completion_kernel,
        grid_spec=pltpu.PrefetchScalarGridSpec(
            num_scalar_prefetch=1,
            grid=(KEY_VALUE_HEADS,),
            in_specs=[
                lane_block(rows, wide),
                lane_block(rows, wide),
                lane_block(total, HEAD_SIZE),
                lane_block(total, HEAD_SIZE, KEY_VALUE_HEADS),
                lane_block(rows, HEAD_SIZE),
                lane_block(rows, HEAD_SIZE, KEY_VALUE_HEADS),
            ],
            out_specs=[
                lane_block(rows, wide),
                lane_block(total, HEAD_SIZE),
                lane_block(total, HEAD_SIZE),
                lane_block(rows, HEAD_SIZE),
                lane_block(rows, HEAD_SIZE),
            ],
            scratch_shapes=[
                pltpu.VMEM((total + rows, GROUP * rows), jnp.bfloat16),
                pltpu.VMEM((total + rows, GROUP * rows), jnp.bfloat16),
            ],
        ),
        out_shape=[
            jax.ShapeDtypeStruct(query.shape, jnp.bfloat16),
            jax.ShapeDtypeStruct((total, HALF), jnp.bfloat16),
            jax.ShapeDtypeStruct((total, HALF), jnp.bfloat16),
            jax.ShapeDtypeStruct((rows, HALF), jnp.bfloat16),
            jax.ShapeDtypeStruct((rows, HALF), jnp.bfloat16),
        ],
        compiler_params=params(),
        name="completion_attention",
    )(length, query, cotangent, kv, kv, own_kv, own_kv)


def local(prompt_query, prompt_kv, prompt_cot, comp_query, comp_kv, comp_cot, group_of, lengths):
    ctx_count = lax.axis_size("ctx")
    comp_count = lax.axis_size("comp")
    ctx_place = lax.axis_index("ctx")
    comp_place = lax.axis_index("comp")
    prompt_rows = prompt_query.shape[1]
    whole_prompt = lax.all_gather(prompt_kv[0], "ctx", axis=0, tiled=True)
    column_groups = jnp.take(group_of.reshape(ctx_count, comp_count), comp_place, axis=1)
    stacked_blocks = lax.all_gather(prompt_kv, "comp", axis=0, tiled=True)
    outgoing = jnp.take(stacked_blocks, column_groups, axis=0)
    incoming = lax.all_to_all(outgoing, "ctx", split_axis=0, concat_axis=0, tiled=True)
    group_prompt = incoming.reshape(-1, incoming.shape[2])
    length = lax.dynamic_slice_in_dim(lengths, ctx_place * comp_count + comp_place, 1)
    comp_dq, comp_dk, comp_dv, own_dk, own_dv = completion_attention(
        comp_query[0], comp_cot[0], group_prompt, comp_kv[0], length
    )
    prompt_dq, prompt_dk, prompt_dv = prompt_attention(
        prompt_query[0], prompt_cot[0], whole_prompt, ctx_place.reshape(1)
    )
    comp_terms = jnp.concatenate([comp_dk, comp_dv], axis=1)
    prompt_terms = jnp.concatenate([prompt_dk, prompt_dv], axis=1)
    outgoing_terms = comp_terms.reshape(ctx_count, prompt_rows, 2 * HALF)
    returned = lax.all_to_all(outgoing_terms, "ctx", split_axis=0, concat_axis=0, tiled=True)
    chooser = column_groups[:, None] == jnp.arange(comp_count, dtype=jnp.int32)[None, :]
    group_table = jnp.einsum(
        "sg,srw->grw",
        chooser.astype(jnp.bfloat16),
        returned,
        preferred_element_type=jnp.float32,
    )
    own_terms = lax.psum_scatter(prompt_terms, "ctx", scatter_dimension=0, tiled=True)
    group_sum = lax.psum_scatter(
        group_table.astype(jnp.bfloat16), "comp", scatter_dimension=0, tiled=True
    )[0]
    summed = group_sum.astype(jnp.float32) + own_terms.astype(jnp.float32)
    return (
        prompt_dq[None],
        summed.astype(jnp.bfloat16)[None],
        comp_dq[None],
        jnp.concatenate([own_dk, own_dv], axis=1)[None],
    )


def solution(mesh):
    placed = (
        P("comp", "ctx", None),
        P("comp", "ctx", None),
        P("comp", "ctx", None),
        P(("ctx", "comp"), None, None),
        P(("ctx", "comp"), None, None),
        P(("ctx", "comp"), None, None),
        P(),
        P(),
    )
    return jax.shard_map(
        local,
        mesh=mesh,
        in_specs=placed,
        out_specs=(
            P("comp", "ctx", None),
            P("comp", "ctx", None),
            P(("ctx", "comp"), None, None),
            P(("ctx", "comp"), None, None),
        ),
        check_vma=False,
    )
```

```python
import functools
import math

import jax
import jax.numpy as jnp
from jax import lax
from jax.experimental import pallas as pl
from jax.experimental.pallas import tpu as pltpu
from jax.sharding import PartitionSpec as P

QUERY_HEADS = 32
KEY_VALUE_HEADS = 4
HEAD_SIZE = 128
GROUP = QUERY_HEADS // KEY_VALUE_HEADS
HALF = KEY_VALUE_HEADS * HEAD_SIZE
PAIR = 2
SCALING = 1.0 / math.sqrt(HEAD_SIZE)

MASK_FILL = -1e30


def heads_to_rows(block, first, count):
    parts = [block[:, (first + i) * HEAD_SIZE : (first + i + 1) * HEAD_SIZE] for i in range(count)]
    return jnp.concatenate(parts, axis=0)


def head_gradients(query, cotangent, keys, values, bias, prob_ref, grad_ref, dq_ref):
    exponent = SCALING * math.log2(math.e)
    rows = query.shape[0]
    for pair in range(GROUP // PAIR):
        q = heads_to_rows(query, pair * PAIR, PAIR)
        c = heads_to_rows(cotangent, pair * PAIR, PAIR)
        scores = lax.dot_general(
            keys, q, (((1,), (1,)), ((), ())), preferred_element_type=jnp.float32
        )
        scores = bias(scores)
        prob_grad = lax.dot_general(
            values, c, (((1,), (1,)), ((), ())), preferred_element_type=jnp.float32
        )
        row_max = jnp.max(scores, axis=0, keepdims=True)
        weights = jnp.exp2((scores - row_max) * exponent)
        inverse = 1.0 / jnp.sum(weights, axis=0, keepdims=True)
        delta = jnp.sum(weights * prob_grad, axis=0, keepdims=True) * inverse
        probability = weights * inverse
        score_grad = (probability * (prob_grad - delta)).astype(jnp.bfloat16)
        columns = slice(pair * PAIR * rows, (pair + 1) * PAIR * rows)
        prob_ref[:, columns] = probability.astype(jnp.bfloat16)
        grad_ref[:, columns] = score_grad
        dq = lax.dot_general(
            score_grad, keys, (((0,), (0,)), ((), ())), preferred_element_type=jnp.float32
        )
        dq = (dq * SCALING).astype(jnp.bfloat16)
        for i in range(PAIR):
            at = (pair * PAIR + i) * HEAD_SIZE
            dq_ref[:, at : at + HEAD_SIZE] = dq[i * rows : (i + 1) * rows]
    key_grad = jnp.dot(
        grad_ref[...], heads_to_rows(query, 0, GROUP), preferred_element_type=jnp.float32
    )
    value_grad = jnp.dot(
        prob_ref[...], heads_to_rows(cotangent, 0, GROUP), preferred_element_type=jnp.float32
    )
    return (key_grad * SCALING).astype(jnp.bfloat16), value_grad.astype(jnp.bfloat16)


def remote(source, target, send, receive, ctx, comp):
    return pltpu.make_async_remote_copy(
        src_ref=source,
        dst_ref=target,
        send_sem=send,
        recv_sem=receive,
        device_id=(ctx, comp),
        device_id_type=pl.DeviceIdType.MESH,
    )


def greet(devices):
    barrier = pltpu.get_barrier_semaphore()
    for device in devices:
        pl.semaphore_signal(
            barrier, inc=1, device_id=device, device_id_type=pl.DeviceIdType.MESH
        )
    pl.semaphore_wait(barrier, len(devices))


def prompt_kernel(
    ctx_count, comp_count, q_ref, c_ref, kv_ref, dq_ref, dk_ref, dv_ref, all_ref,
    whole, bias_ref, prob_ref, grad_ref,
    up_send, up_recv, down_send, down_recv, pair_send, pair_recv,
    side_send, side_recv, pass_send, pass_recv, keep_sem,
):
    step = pl.program_id(0)
    place = lax.axis_index("ctx")
    column = lax.axis_index("comp")
    rows = q_ref.shape[0]
    total = ctx_count * rows
    chips = ctx_count // 2
    chip, core = place // 2, place % 2
    sibling = chip * 2 + 1 - core

    def other(offset):
        return (column + offset) % comp_count

    def up(t):
        at = (chip - t) * 2 + core
        return remote(whole.at[at], whole.at[at], up_send.at[t], up_recv.at[t], place + 2, column)

    def up_arrival(t):
        at = (chip - 1 - t) * 2 + core
        return remote(whole.at[at], whole.at[at], up_send.at[t], up_recv.at[t], place - 2, column)

    def down(t):
        at = (chip + t) * 2 + core
        return remote(
            whole.at[at], whole.at[at], down_send.at[t], down_recv.at[t], place - 2, column
        )

    def down_arrival(t):
        at = (chip + 1 + t) * 2 + core
        return remote(
            whole.at[at], whole.at[at], down_send.at[t], down_recv.at[t], place + 2, column
        )

    def to_sibling(k, side):
        at = k * 2 + side
        return remote(
            whole.at[at], whole.at[at], pair_send.at[k], pair_recv.at[k], sibling, column
        )

    def to_column(k, e):
        at = k * 2 + core
        return remote(
            whole.at[at],
            all_ref.at[column, at],
            side_send.at[e - 1, k],
            side_recv.at[e - 1, k],
            place,
            other(e),
        )

    def from_column(k, e):
        at = k * 2 + core
        source = other(comp_count - e)
        return remote(
            whole.at[at],
            all_ref.at[source, at],
            side_send.at[e - 1, k],
            side_recv.at[e - 1, k],
            place,
            source,
        )

    def pass_on(k, e, side):
        at = k * 2 + side
        source = other(comp_count - e)
        return remote(
            all_ref.at[source, at],
            all_ref.at[source, at],
            pass_send.at[e - 1, k],
            pass_recv.at[e - 1, k],
            sibling,
            column,
        )

    keep = pltpu.make_async_copy(whole, all_ref.at[column], keep_sem)

    def share(k):
        to_sibling(k, core).start()
        for e in range(1, comp_count):
            to_column(k, e).start()

    @pl.when(step == 0)
    def _():
        whole[place] = kv_ref[...]
        greetings = [(sibling, column)]
        greetings += [(place, other(e)) for e in range(1, comp_count)]
        greet(greetings + [
            ((place + 2) % ctx_count, column),
            ((place + ctx_count - 2) % ctx_count, column),
        ])
        for t in range(chips - 1):

            @pl.when((chip - t >= 0) & (chip + 1 < chips))
            def _():
                up(t).start()

            @pl.when((chip + t < chips) & (chip >= 1))
            def _():
                down(t).start()

            if t == 0:
                share(chip)

            @pl.when(chip - 1 - t >= 0)
            def _():
                up_arrival(t).wait_recv()
                share(chip - 1 - t)

            @pl.when(chip + 1 + t < chips)
            def _():
                down_arrival(t).wait_recv()
                share(chip + 1 + t)

        for k in range(chips):
            to_sibling(k, 1 - core).wait_recv()
        keep.start()
        shape = (total, rows)
        key_at = lax.broadcasted_iota(jnp.int32, shape, 0)
        row_at = lax.broadcasted_iota(jnp.int32, shape, 1)
        bias_ref[...] = jnp.where(key_at <= row_at + place * rows, 0.0, MASK_FILL)

    def bias(scores):
        return scores + jnp.concatenate([bias_ref[...]] * PAIR, axis=1)

    def head_of(shift):
        at = pl.multiple_of((step + shift) * HEAD_SIZE, HEAD_SIZE)
        return whole[:, :, pl.ds(at, HEAD_SIZE)].reshape(total, HEAD_SIZE)

    dk, dv = head_gradients(
        q_ref[...], c_ref[...], head_of(0), head_of(KEY_VALUE_HEADS), bias,
        prob_ref, grad_ref, dq_ref,
    )
    dk_ref[...] = dk
    dv_ref[...] = dv

    for r in range(chips):

        @pl.when(step == r % KEY_VALUE_HEADS)
        def _():
            k = (chip + r) % chips
            for e in range(1, comp_count):
                from_column(k, e).wait_recv()
                pass_on(k, e, core).start()

    @pl.when(step == KEY_VALUE_HEADS - 1)
    def _():
        for t in range(chips - 1):

            @pl.when((chip - t >= 0) & (chip + 1 < chips))
            def _():
                up(t).wait_send()

            @pl.when((chip + t < chips) & (chip >= 1))
            def _():
                down(t).wait_send()

        for k in range(chips):
            to_sibling(k, core).wait_send()
            for e in range(1, comp_count):
                to_column(k, e).wait_send()
                pass_on(k, e, core).wait_send()
                pass_on(k, e, 1 - core).wait_recv()
        keep.wait()


def completion_kernel(
    ctx_count, comp_count, length_ref, chooser_ref, q_ref, c_ref, k_ref, v_ref, own_k_ref, own_v_ref,
    dq_ref, own_dk_ref, own_dv_ref, sum_ref,
    prob_ref, grad_ref, terms, arrived, table, table_in,
    send, recv, side_send, side_recv,
):
    step = pl.program_id(0)
    place = lax.axis_index("ctx")
    column = lax.axis_index("comp")
    rows = q_ref.shape[0]
    total = k_ref.shape[0]
    part = total // ctx_count
    length = length_ref[0]

    def other(offset):
        return (column + offset) % comp_count

    def out_to(h, d):
        target = (place + d) % ctx_count
        return remote(
            terms.at[h, target], arrived.at[h, d - 1], send.at[h, d - 1], recv.at[h, d - 1],
            target, column,
        )

    def across(h, e):
        return remote(
            table.at[h, e - 1], table_in.at[h, e - 1], side_send.at[h, e - 1],
            side_recv.at[h, e - 1], place, other(e),
        )

    @pl.when(step == 0)
    def _():
        greet(
            [((place + d) % ctx_count, column) for d in range(1, ctx_count)]
            + [(place, other(e)) for e in range(1, comp_count)]
        )

    key_at = lax.broadcasted_iota(jnp.int32, (rows, rows), 0)
    row_at = lax.broadcasted_iota(jnp.int32, (rows, rows), 1)
    own_bias = jnp.where((key_at <= row_at) & (key_at < length), 0.0, MASK_FILL)

    def bias(scores):
        own = scores[total:] + jnp.concatenate([own_bias] * PAIR, axis=1)
        return jnp.concatenate([scores[:total], own], axis=0)

    cotangent = c_ref[...]
    live = lax.broadcasted_iota(jnp.int32, cotangent.shape, 0) < length
    cotangent = jnp.where(live, cotangent, jnp.zeros_like(cotangent))
    keys = jnp.concatenate([k_ref[...], own_k_ref[...]], axis=0)
    values = jnp.concatenate([v_ref[...], own_v_ref[...]], axis=0)
    dk, dv = head_gradients(q_ref[...], cotangent, keys, values, bias, prob_ref, grad_ref, dq_ref)
    terms[step, :, :, :HEAD_SIZE] = dk[:total].reshape(ctx_count, part, HEAD_SIZE)
    terms[step, :, :, HEAD_SIZE:] = dv[:total].reshape(ctx_count, part, HEAD_SIZE)
    for d in range(1, ctx_count):
        out_to(step, d).start()
    own_dk_ref[...] = dk[total:]
    own_dv_ref[...] = dv[total:]

    @pl.when(step == KEY_VALUE_HEADS - 1)
    def _():
        def reduce_head(h, carry):
            for d in range(1, ctx_count):
                out_to(h, d).wait_recv()
            for e in list(range(1, comp_count)) + [0]:
                summed = terms[h, place].astype(jnp.float32) * chooser_ref[place, other(e)]
                for d in range(1, ctx_count):
                    source = (place + ctx_count - d) % ctx_count
                    weight = chooser_ref[source, other(e)]
                    summed += arrived[h, d - 1].astype(jnp.float32) * weight
                if e:
                    table[h, e - 1] = summed.astype(jnp.bfloat16)
                    across(h, e).start()
                else:
                    sum_ref[h] = summed
            return carry

        def finish_head(h, carry):
            summed = sum_ref[h]
            for e in range(1, comp_count):
                across(h, e).wait_recv()
                summed += table_in[h, e - 1].astype(jnp.float32)
            sum_ref[h] = summed
            for e in range(1, comp_count):
                across(h, e).wait_send()
            for d in range(1, ctx_count):
                out_to(h, d).wait_send()
            return carry

        lax.fori_loop(0, KEY_VALUE_HEADS, reduce_head, 0)
        lax.fori_loop(0, KEY_VALUE_HEADS, finish_head, 0)


def lane_block(rows, width, shift=0):
    return pl.BlockSpec((rows, width), lambda h: (0, h + shift))


def params(collective_id):
    return pltpu.CompilerParams(
        vmem_limit_bytes=56 * 1024 * 1024, collective_id=collective_id, has_side_effects=True
    )


def prompt_attention(query, cotangent, kv):
    ctx_count, comp_count = lax.axis_size("ctx"), lax.axis_size("comp")
    rows = query.shape[0]
    total = rows * ctx_count
    chips = ctx_count // 2
    wide = GROUP * HEAD_SIZE
    dma = pltpu.SemaphoreType.DMA
    return pl.pallas_call(
        functools.partial(prompt_kernel, ctx_count, comp_count),
        grid=(KEY_VALUE_HEADS,),
        in_specs=[
            lane_block(rows, wide),
            lane_block(rows, wide),
            pl.BlockSpec(kv.shape, lambda h: (0, 0)),
        ],
        out_specs=[
            lane_block(rows, wide),
            lane_block(total, HEAD_SIZE),
            lane_block(total, HEAD_SIZE),
            pl.BlockSpec(memory_space=pl.ANY),
        ],
        scratch_shapes=[
            pltpu.VMEM((ctx_count, rows, 2 * HALF), jnp.bfloat16),
            pltpu.VMEM((total, rows), jnp.float32),
            pltpu.VMEM((total, GROUP * rows), jnp.bfloat16),
            pltpu.VMEM((total, GROUP * rows), jnp.bfloat16),
        ]
        + [dma((chips - 1,))] * 4
        + [dma((chips,))] * 2
        + [dma((comp_count - 1, chips))] * 4
        + [dma],
        out_shape=[
            jax.ShapeDtypeStruct(query.shape, jnp.bfloat16),
            jax.ShapeDtypeStruct((total, HALF), jnp.bfloat16),
            jax.ShapeDtypeStruct((total, HALF), jnp.bfloat16),
            jax.ShapeDtypeStruct((comp_count, ctx_count, rows, 2 * HALF), jnp.bfloat16),
        ],
        compiler_params=params(1),
        name="prompt_attention",
    )(query, cotangent, kv)


def completion_attention(query, cotangent, kv, own_kv, length, chooser):
    ctx_count, comp_count = lax.axis_size("ctx"), lax.axis_size("comp")
    rows, total = query.shape[0], kv.shape[0]
    part = total // ctx_count
    wide = GROUP * HEAD_SIZE
    dma = pltpu.SemaphoreType.DMA
    sums = (KEY_VALUE_HEADS, part, 2 * HEAD_SIZE)
    return pl.pallas_call(
        functools.partial(completion_kernel, ctx_count, comp_count),
        grid=(KEY_VALUE_HEADS,),
        in_specs=[
            pl.BlockSpec(memory_space=pltpu.SMEM),
            pl.BlockSpec(memory_space=pltpu.SMEM),
            lane_block(rows, wide),
            lane_block(rows, wide),
            lane_block(total, HEAD_SIZE),
            lane_block(total, HEAD_SIZE, KEY_VALUE_HEADS),
            lane_block(rows, HEAD_SIZE),
            lane_block(rows, HEAD_SIZE, KEY_VALUE_HEADS),
        ],
        out_specs=[
            lane_block(rows, wide),
            lane_block(rows, HEAD_SIZE),
            lane_block(rows, HEAD_SIZE),
            pl.BlockSpec(sums, lambda h: (0, 0, 0)),
        ],
        scratch_shapes=[
            pltpu.VMEM((total + rows, GROUP * rows), jnp.bfloat16),
            pltpu.VMEM((total + rows, GROUP * rows), jnp.bfloat16),
            pltpu.VMEM((KEY_VALUE_HEADS, ctx_count, part, 2 * HEAD_SIZE), jnp.bfloat16),
            pltpu.VMEM((KEY_VALUE_HEADS, ctx_count - 1, part, 2 * HEAD_SIZE), jnp.bfloat16),
            pltpu.VMEM((KEY_VALUE_HEADS, comp_count - 1, part, 2 * HEAD_SIZE), jnp.bfloat16),
            pltpu.VMEM((KEY_VALUE_HEADS, comp_count - 1, part, 2 * HEAD_SIZE), jnp.bfloat16),
            dma((KEY_VALUE_HEADS, ctx_count - 1)),
            dma((KEY_VALUE_HEADS, ctx_count - 1)),
            dma((KEY_VALUE_HEADS, comp_count - 1)),
            dma((KEY_VALUE_HEADS, comp_count - 1)),
        ],
        out_shape=[
            jax.ShapeDtypeStruct(query.shape, jnp.bfloat16),
            jax.ShapeDtypeStruct((rows, HALF), jnp.bfloat16),
            jax.ShapeDtypeStruct((rows, HALF), jnp.bfloat16),
            jax.ShapeDtypeStruct(sums, jnp.float32),
        ],
        compiler_params=params(2),
        name="completion_attention",
    )(length, chooser, query, cotangent, kv, kv, own_kv, own_kv)


def local(prompt_query, prompt_kv, prompt_cot, comp_query, comp_kv, comp_cot, group_of, lengths):
    ctx_count = lax.axis_size("ctx")
    comp_count = lax.axis_size("comp")
    ctx_place = lax.axis_index("ctx")
    comp_place = lax.axis_index("comp")
    column_groups = jnp.take(group_of.reshape(ctx_count, comp_count), comp_place, axis=1)
    chooser = column_groups[:, None] == jnp.arange(comp_count, dtype=jnp.int32)[None, :]
    length = lax.dynamic_slice_in_dim(lengths, ctx_place * comp_count + comp_place, 1)
    prompt_dq, prompt_dk, prompt_dv, prompts = prompt_attention(
        prompt_query[0], prompt_cot[0], prompt_kv[0]
    )
    group_prompt = lax.dynamic_index_in_dim(prompts, column_groups[ctx_place], 0, keepdims=False)
    prompt_terms = jnp.concatenate([prompt_dk, prompt_dv], axis=1)
    own_terms = lax.psum_scatter(prompt_terms, "ctx", scatter_dimension=0, tiled=True)
    comp_dq, own_dk, own_dv, sums = completion_attention(
        comp_query[0],
        comp_cot[0],
        group_prompt.reshape(-1, 2 * HALF),
        comp_kv[0],
        length,
        chooser.astype(jnp.float32),
    )
    sums = jnp.concatenate(
        [sums[h, :, :HEAD_SIZE] for h in range(KEY_VALUE_HEADS)]
        + [sums[h, :, HEAD_SIZE:] for h in range(KEY_VALUE_HEADS)],
        axis=1,
    )
    summed = sums + own_terms.astype(jnp.float32)
    return (
        prompt_dq[None],
        summed.astype(jnp.bfloat16)[None],
        comp_dq[None],
        jnp.concatenate([own_dk, own_dv], axis=1)[None],
    )


def solution(mesh):
    placed = (
        P("comp", "ctx", None),
        P("comp", "ctx", None),
        P("comp", "ctx", None),
        P(("ctx", "comp"), None, None),
        P(("ctx", "comp"), None, None),
        P(("ctx", "comp"), None, None),
        P(),
        P(),
    )
    return jax.shard_map(
        local,
        mesh=mesh,
        in_specs=placed,
        out_specs=(
            P("comp", "ctx", None),
            P("comp", "ctx", None),
            P(("ctx", "comp"), None, None),
            P(("ctx", "comp"), None, None),
        ),
        check_vma=False,
    )
```

```python
import functools
import math

import jax
import jax.numpy as jnp
from jax import lax
from jax.experimental import pallas as pl
from jax.experimental.pallas import tpu as pltpu
from jax.sharding import PartitionSpec as P

QUERY_HEADS = 32
KEY_VALUE_HEADS = 4
HEAD_SIZE = 128
GROUP = QUERY_HEADS // KEY_VALUE_HEADS
HALF = KEY_VALUE_HEADS * HEAD_SIZE
PAIR = 2
SCALING = 1.0 / math.sqrt(HEAD_SIZE)

MASK_FILL = -1e30


def heads_to_rows(block, first, count):
    parts = [block[:, (first + i) * HEAD_SIZE : (first + i + 1) * HEAD_SIZE] for i in range(count)]
    return jnp.concatenate(parts, axis=0)


def head_gradients(query, cotangent, keys, values, bias, prob_ref, grad_ref, dq_ref):
    exponent = SCALING * math.log2(math.e)
    rows = query.shape[0]
    for pair in range(GROUP // PAIR):
        q = heads_to_rows(query, pair * PAIR, PAIR)
        c = heads_to_rows(cotangent, pair * PAIR, PAIR)
        scores = lax.dot_general(
            keys, q, (((1,), (1,)), ((), ())), preferred_element_type=jnp.float32
        )
        scores = bias(scores)
        prob_grad = lax.dot_general(
            values, c, (((1,), (1,)), ((), ())), preferred_element_type=jnp.float32
        )
        row_max = jnp.max(scores, axis=0, keepdims=True)
        weights = jnp.exp2((scores - row_max) * exponent)
        inverse = 1.0 / jnp.sum(weights, axis=0, keepdims=True)
        delta = jnp.sum(weights * prob_grad, axis=0, keepdims=True) * inverse
        probability = weights * inverse
        score_grad = (probability * (prob_grad - delta)).astype(jnp.bfloat16)
        columns = slice(pair * PAIR * rows, (pair + 1) * PAIR * rows)
        prob_ref[:, columns] = probability.astype(jnp.bfloat16)
        grad_ref[:, columns] = score_grad
        dq = lax.dot_general(
            score_grad, keys, (((0,), (0,)), ((), ())), preferred_element_type=jnp.float32
        )
        dq = (dq * SCALING).astype(jnp.bfloat16)
        for i in range(PAIR):
            at = (pair * PAIR + i) * HEAD_SIZE
            dq_ref[:, at : at + HEAD_SIZE] = dq[i * rows : (i + 1) * rows]
    key_grad = jnp.dot(
        grad_ref[...], heads_to_rows(query, 0, GROUP), preferred_element_type=jnp.float32
    )
    value_grad = jnp.dot(
        prob_ref[...], heads_to_rows(cotangent, 0, GROUP), preferred_element_type=jnp.float32
    )
    return (key_grad * SCALING).astype(jnp.bfloat16), value_grad.astype(jnp.bfloat16)


def remote(source, target, send, receive, ctx, comp):
    return pltpu.make_async_remote_copy(
        src_ref=source,
        dst_ref=target,
        send_sem=send,
        recv_sem=receive,
        device_id=(ctx, comp),
        device_id_type=pl.DeviceIdType.MESH,
    )


def greet(devices):
    barrier = pltpu.get_barrier_semaphore()
    for device in devices:
        pl.semaphore_signal(
            barrier, inc=1, device_id=device, device_id_type=pl.DeviceIdType.MESH
        )
    pl.semaphore_wait(barrier, len(devices))


def lanes_of(head):
    return [
        pl.ds(pl.multiple_of((head + shift) * HEAD_SIZE, HEAD_SIZE), HEAD_SIZE)
        for shift in (0, KEY_VALUE_HEADS)
    ]


def prompt_kernel(
    ctx_count, comp_count, q_ref, c_ref, kv_ref, dq_ref, own_ref, all_ref,
    whole, bias_ref, prob_ref, grad_ref, terms, pair_in, chip_terms, chip_in,
    up_send, up_recv, down_send, down_recv, pair_send, pair_recv,
    side_send, side_recv, pass_send, pass_recv, keep_sem,
    half_send, half_recv, term_send, term_recv,
):
    step = pl.program_id(0)
    place = lax.axis_index("ctx")
    column = lax.axis_index("comp")
    rows = q_ref.shape[0]
    total = ctx_count * rows
    chips = ctx_count // 2
    chip, core = place // 2, place % 2
    sibling = chip * 2 + 1 - core

    def other(offset):
        return (column + offset) % comp_count

    def up(t):
        at = (chip - t) * 2 + core
        return remote(whole.at[at], whole.at[at], up_send.at[t], up_recv.at[t], place + 2, column)

    def up_arrival(t):
        at = (chip - 1 - t) * 2 + core
        return remote(whole.at[at], whole.at[at], up_send.at[t], up_recv.at[t], place - 2, column)

    def down(t):
        at = (chip + t) * 2 + core
        return remote(
            whole.at[at], whole.at[at], down_send.at[t], down_recv.at[t], place - 2, column
        )

    def down_arrival(t):
        at = (chip + 1 + t) * 2 + core
        return remote(
            whole.at[at], whole.at[at], down_send.at[t], down_recv.at[t], place + 2, column
        )

    def to_sibling(k, side):
        at = k * 2 + side
        return remote(
            whole.at[at], whole.at[at], pair_send.at[k], pair_recv.at[k], sibling, column
        )

    def to_column(k, e):
        at = k * 2 + core
        return remote(
            whole.at[at],
            all_ref.at[column, at],
            side_send.at[e - 1, k],
            side_recv.at[e - 1, k],
            place,
            other(e),
        )

    def from_column(k, e):
        at = k * 2 + core
        source = other(comp_count - e)
        return remote(
            whole.at[at],
            all_ref.at[source, at],
            side_send.at[e - 1, k],
            side_recv.at[e - 1, k],
            place,
            source,
        )

    def pass_on(k, e, side):
        at = k * 2 + side
        source = other(comp_count - e)
        return remote(
            all_ref.at[source, at],
            all_ref.at[source, at],
            pass_send.at[e - 1, k],
            pass_recv.at[e - 1, k],
            sibling,
            column,
        )

    def half_over(h):
        return remote(
            terms.at[h, 1 - core], pair_in.at[h], half_send.at[h], half_recv.at[h], sibling, column
        )

    def terms_to(h, d):
        target = (chip + d) % chips
        return remote(
            chip_terms.at[h, target], chip_in.at[h, d - 1], term_send.at[h, d - 1],
            term_recv.at[h, d - 1], target * 2 + core, column,
        )

    def send_chip_terms(h):
        half_over(h).wait_recv()
        summed = terms[h, core].astype(jnp.float32) + pair_in[h].astype(jnp.float32)
        chip_terms[h] = summed.astype(jnp.bfloat16)
        for d in range(1, chips):
            terms_to(h, d).start()

    keep = pltpu.make_async_copy(whole, all_ref.at[column], keep_sem)

    def share(k):
        to_sibling(k, core).start()
        for e in range(1, comp_count):
            to_column(k, e).start()

    @pl.when(step == 0)
    def _():
        whole[place] = kv_ref[...]
        greetings = [(sibling, column)]
        greetings += [(place, other(e)) for e in range(1, comp_count)]
        greet(
            greetings + [((place + 2 * d) % ctx_count, column) for d in range(1, chips)]
        )
        for t in range(chips - 1):

            @pl.when((chip - t >= 0) & (chip + 1 < chips))
            def _():
                up(t).start()

            @pl.when((chip + t < chips) & (chip >= 1))
            def _():
                down(t).start()

            if t == 0:
                share(chip)

            @pl.when(chip - 1 - t >= 0)
            def _():
                up_arrival(t).wait_recv()
                share(chip - 1 - t)

            @pl.when(chip + 1 + t < chips)
            def _():
                down_arrival(t).wait_recv()
                share(chip + 1 + t)

        for k in range(chips):
            to_sibling(k, 1 - core).wait_recv()
        keep.start()
        shape = (total, rows)
        key_at = lax.broadcasted_iota(jnp.int32, shape, 0)
        row_at = lax.broadcasted_iota(jnp.int32, shape, 1)
        bias_ref[...] = jnp.where(key_at <= row_at + place * rows, 0.0, MASK_FILL)

    def bias(scores):
        return scores + jnp.concatenate([bias_ref[...]] * PAIR, axis=1)

    def head_of(shift):
        at = pl.multiple_of((step + shift) * HEAD_SIZE, HEAD_SIZE)
        return whole[:, :, pl.ds(at, HEAD_SIZE)].reshape(total, HEAD_SIZE)

    dk, dv = head_gradients(
        q_ref[...], c_ref[...], head_of(0), head_of(KEY_VALUE_HEADS), bias,
        prob_ref, grad_ref, dq_ref,
    )
    dk = dk.reshape(chips, 2, rows, HEAD_SIZE)
    dv = dv.reshape(chips, 2, rows, HEAD_SIZE)
    for side in range(2):
        terms[step, side, :, :, :HEAD_SIZE] = dk[:, side]
        terms[step, side, :, :, HEAD_SIZE:] = dv[:, side]
    half_over(step).start()

    @pl.when(step >= 1)
    def _():
        send_chip_terms(step - 1)

    for r in range(chips):

        @pl.when(step == r % KEY_VALUE_HEADS)
        def _():
            k = (chip + r) % chips
            for e in range(1, comp_count):
                from_column(k, e).wait_recv()
                pass_on(k, e, core).start()

    @pl.when(step == KEY_VALUE_HEADS - 1)
    def _():
        send_chip_terms(KEY_VALUE_HEADS - 1)
        for h in range(KEY_VALUE_HEADS):
            half_over(h).wait_send()
            summed = chip_terms[h, chip].astype(jnp.float32)
            for d in range(1, chips):
                terms_to(h, d).wait_recv()
                summed += chip_in[h, d - 1].astype(jnp.float32)
            own_ref[:, h * HEAD_SIZE : (h + 1) * HEAD_SIZE] = summed[:, :HEAD_SIZE]
            own_ref[:, HALF + h * HEAD_SIZE : HALF + (h + 1) * HEAD_SIZE] = summed[:, HEAD_SIZE:]
            for d in range(1, chips):
                terms_to(h, d).wait_send()

        for t in range(chips - 1):

            @pl.when((chip - t >= 0) & (chip + 1 < chips))
            def _():
                up(t).wait_send()

            @pl.when((chip + t < chips) & (chip >= 1))
            def _():
                down(t).wait_send()

        for k in range(chips):
            to_sibling(k, core).wait_send()
            for e in range(1, comp_count):
                to_column(k, e).wait_send()
                pass_on(k, e, core).wait_send()
                pass_on(k, e, 1 - core).wait_recv()
        keep.wait()


def completion_kernel(
    ctx_count, comp_count, length_ref, chooser_ref, q_ref, c_ref, k_ref, v_ref, own_k_ref, own_v_ref,
    prompt_ref, dq_ref, own_ref, out_ref,
    sum_ref, prob_ref, grad_ref, terms, arrived, table, table_in,
    send, recv, side_send, side_recv,
):
    step = pl.program_id(0)
    place = lax.axis_index("ctx")
    column = lax.axis_index("comp")
    rows = q_ref.shape[0]
    total = k_ref.shape[0]
    part = total // ctx_count
    length = length_ref[0]

    def other(offset):
        return (column + offset) % comp_count

    def out_to(h, d):
        target = (place + d) % ctx_count
        return remote(
            terms.at[h, target], arrived.at[h, d - 1], send.at[h, d - 1], recv.at[h, d - 1],
            target, column,
        )

    def across(h, e):
        return remote(
            table.at[h, e - 1], table_in.at[h, e - 1], side_send.at[h, e - 1],
            side_recv.at[h, e - 1], place, other(e),
        )

    @pl.when(step == 0)
    def _():
        greet(
            [((place + d) % ctx_count, column) for d in range(1, ctx_count)]
            + [(place, other(e)) for e in range(1, comp_count)]
        )

    key_at = lax.broadcasted_iota(jnp.int32, (rows, rows), 0)
    row_at = lax.broadcasted_iota(jnp.int32, (rows, rows), 1)
    own_bias = jnp.where((key_at <= row_at) & (key_at < length), 0.0, MASK_FILL)

    def bias(scores):
        own = scores[total:] + jnp.concatenate([own_bias] * PAIR, axis=1)
        return jnp.concatenate([scores[:total], own], axis=0)

    cotangent = c_ref[...]
    live = lax.broadcasted_iota(jnp.int32, cotangent.shape, 0) < length
    cotangent = jnp.where(live, cotangent, jnp.zeros_like(cotangent))
    keys = jnp.concatenate([k_ref[...], own_k_ref[...]], axis=0)
    values = jnp.concatenate([v_ref[...], own_v_ref[...]], axis=0)
    dk, dv = head_gradients(q_ref[...], cotangent, keys, values, bias, prob_ref, grad_ref, dq_ref)
    terms[step, :, :, :HEAD_SIZE] = dk[:total].reshape(ctx_count, part, HEAD_SIZE)
    terms[step, :, :, HEAD_SIZE:] = dv[:total].reshape(ctx_count, part, HEAD_SIZE)
    for d in range(1, ctx_count):
        out_to(step, d).start()
    key_lanes, value_lanes = lanes_of(step)
    own_ref[:, key_lanes] = dk[total:]
    own_ref[:, value_lanes] = dv[total:]

    @pl.when(step == KEY_VALUE_HEADS - 1)
    def _():
        def reduce_head(h, carry):
            for d in range(1, ctx_count):
                out_to(h, d).wait_recv()
            for e in list(range(1, comp_count)) + [0]:
                summed = terms[h, place].astype(jnp.float32) * chooser_ref[place, other(e)]
                for d in range(1, ctx_count):
                    source = (place + ctx_count - d) % ctx_count
                    weight = chooser_ref[source, other(e)]
                    summed += arrived[h, d - 1].astype(jnp.float32) * weight
                if e:
                    table[h, e - 1] = summed.astype(jnp.bfloat16)
                    across(h, e).start()
                else:
                    sum_ref[h] = summed
            return carry

        def finish_head(h, carry):
            summed = sum_ref[h]
            for e in range(1, comp_count):
                across(h, e).wait_recv()
                summed += table_in[h, e - 1].astype(jnp.float32)
            for at, lanes in enumerate(lanes_of(h)):
                part_sum = summed[:, at * HEAD_SIZE : (at + 1) * HEAD_SIZE]
                out_ref[:, lanes] = (part_sum + prompt_ref[:, lanes]).astype(jnp.bfloat16)
            for e in range(1, comp_count):
                across(h, e).wait_send()
            for d in range(1, ctx_count):
                out_to(h, d).wait_send()
            return carry

        lax.fori_loop(0, KEY_VALUE_HEADS, reduce_head, 0)
        lax.fori_loop(0, KEY_VALUE_HEADS, finish_head, 0)


def lane_block(rows, width, shift=0):
    return pl.BlockSpec((rows, width), lambda h: (0, h + shift))


def params(collective_id):
    return pltpu.CompilerParams(
        vmem_limit_bytes=56 * 1024 * 1024, collective_id=collective_id, has_side_effects=True
    )


def prompt_attention(query, cotangent, kv):
    ctx_count, comp_count = lax.axis_size("ctx"), lax.axis_size("comp")
    rows = query.shape[0]
    total = rows * ctx_count
    chips = ctx_count // 2
    wide = GROUP * HEAD_SIZE
    dma = pltpu.SemaphoreType.DMA
    return pl.pallas_call(
        functools.partial(prompt_kernel, ctx_count, comp_count),
        grid=(KEY_VALUE_HEADS,),
        in_specs=[
            lane_block(rows, wide),
            lane_block(rows, wide),
            pl.BlockSpec(kv.shape, lambda h: (0, 0)),
        ],
        out_specs=[
            lane_block(rows, wide),
            pl.BlockSpec(kv.shape, lambda h: (0, 0)),
            pl.BlockSpec(memory_space=pl.ANY),
        ],
        scratch_shapes=[
            pltpu.VMEM((ctx_count, rows, 2 * HALF), jnp.bfloat16),
            pltpu.VMEM((total, rows), jnp.float32),
            pltpu.VMEM((total, GROUP * rows), jnp.bfloat16),
            pltpu.VMEM((total, GROUP * rows), jnp.bfloat16),
            pltpu.VMEM((KEY_VALUE_HEADS, 2, chips, rows, 2 * HEAD_SIZE), jnp.bfloat16),
            pltpu.VMEM((KEY_VALUE_HEADS, chips, rows, 2 * HEAD_SIZE), jnp.bfloat16),
            pltpu.VMEM((KEY_VALUE_HEADS, chips, rows, 2 * HEAD_SIZE), jnp.bfloat16),
            pltpu.VMEM((KEY_VALUE_HEADS, chips - 1, rows, 2 * HEAD_SIZE), jnp.bfloat16),
        ]
        + [dma((chips - 1,))] * 4
        + [dma((chips,))] * 2
        + [dma((comp_count - 1, chips))] * 4
        + [dma]
        + [dma((KEY_VALUE_HEADS,))] * 2
        + [dma((KEY_VALUE_HEADS, chips - 1))] * 2,
        out_shape=[
            jax.ShapeDtypeStruct(query.shape, jnp.bfloat16),
            jax.ShapeDtypeStruct(kv.shape, jnp.float32),
            jax.ShapeDtypeStruct((comp_count, ctx_count, rows, 2 * HALF), jnp.bfloat16),
        ],
        compiler_params=params(1),
        name="prompt_attention",
    )(query, cotangent, kv)


def completion_attention(query, cotangent, kv, own_kv, prompt_sum, length, chooser):
    ctx_count, comp_count = lax.axis_size("ctx"), lax.axis_size("comp")
    rows, total = query.shape[0], kv.shape[0]
    part = total // ctx_count
    wide = GROUP * HEAD_SIZE
    dma = pltpu.SemaphoreType.DMA
    sums = (KEY_VALUE_HEADS, part, 2 * HEAD_SIZE)
    return pl.pallas_call(
        functools.partial(completion_kernel, ctx_count, comp_count),
        grid=(KEY_VALUE_HEADS,),
        in_specs=[
            pl.BlockSpec(memory_space=pltpu.SMEM),
            pl.BlockSpec(memory_space=pltpu.SMEM),
            lane_block(rows, wide),
            lane_block(rows, wide),
            lane_block(total, HEAD_SIZE),
            lane_block(total, HEAD_SIZE, KEY_VALUE_HEADS),
            lane_block(rows, HEAD_SIZE),
            lane_block(rows, HEAD_SIZE, KEY_VALUE_HEADS),
            pl.BlockSpec(prompt_sum.shape, lambda h: (0, 0)),
        ],
        out_specs=[
            lane_block(rows, wide),
            pl.BlockSpec(own_kv.shape, lambda h: (0, 0)),
            pl.BlockSpec(prompt_sum.shape, lambda h: (0, 0)),
        ],
        scratch_shapes=[
            pltpu.VMEM(sums, jnp.float32),
            pltpu.VMEM((total + rows, GROUP * rows), jnp.bfloat16),
            pltpu.VMEM((total + rows, GROUP * rows), jnp.bfloat16),
            pltpu.VMEM((KEY_VALUE_HEADS, ctx_count, part, 2 * HEAD_SIZE), jnp.bfloat16),
            pltpu.VMEM((KEY_VALUE_HEADS, ctx_count - 1, part, 2 * HEAD_SIZE), jnp.bfloat16),
            pltpu.VMEM((KEY_VALUE_HEADS, comp_count - 1, part, 2 * HEAD_SIZE), jnp.bfloat16),
            pltpu.VMEM((KEY_VALUE_HEADS, comp_count - 1, part, 2 * HEAD_SIZE), jnp.bfloat16),
            dma((KEY_VALUE_HEADS, ctx_count - 1)),
            dma((KEY_VALUE_HEADS, ctx_count - 1)),
            dma((KEY_VALUE_HEADS, comp_count - 1)),
            dma((KEY_VALUE_HEADS, comp_count - 1)),
        ],
        out_shape=[
            jax.ShapeDtypeStruct(query.shape, jnp.bfloat16),
            jax.ShapeDtypeStruct(own_kv.shape, jnp.bfloat16),
            jax.ShapeDtypeStruct(prompt_sum.shape, jnp.bfloat16),
        ],
        compiler_params=params(2),
        name="completion_attention",
    )(length, chooser, query, cotangent, kv, kv, own_kv, own_kv, prompt_sum)


def local(prompt_query, prompt_kv, prompt_cot, comp_query, comp_kv, comp_cot, group_of, lengths):
    ctx_count = lax.axis_size("ctx")
    comp_count = lax.axis_size("comp")
    ctx_place = lax.axis_index("ctx")
    comp_place = lax.axis_index("comp")
    column_groups = jnp.take(group_of.reshape(ctx_count, comp_count), comp_place, axis=1)
    chooser = column_groups[:, None] == jnp.arange(comp_count, dtype=jnp.int32)[None, :]
    length = lax.dynamic_slice_in_dim(lengths, ctx_place * comp_count + comp_place, 1)
    prompt_dq, prompt_sum, prompts = prompt_attention(
        prompt_query[0], prompt_cot[0], prompt_kv[0]
    )
    group_prompt = lax.dynamic_index_in_dim(prompts, column_groups[ctx_place], 0, keepdims=False)
    comp_dq, own_dkv, summed = completion_attention(
        comp_query[0],
        comp_cot[0],
        group_prompt.reshape(-1, 2 * HALF),
        comp_kv[0],
        prompt_sum,
        length,
        chooser.astype(jnp.float32),
    )
    return prompt_dq[None], summed[None], comp_dq[None], own_dkv[None]


def solution(mesh):
    placed = (
        P("comp", "ctx", None),
        P("comp", "ctx", None),
        P("comp", "ctx", None),
        P(("ctx", "comp"), None, None),
        P(("ctx", "comp"), None, None),
        P(("ctx", "comp"), None, None),
        P(),
        P(),
    )
    return jax.shard_map(
        local,
        mesh=mesh,
        in_specs=placed,
        out_specs=(
            P("comp", "ctx", None),
            P("comp", "ctx", None),
            P(("ctx", "comp"), None, None),
            P(("ctx", "comp"), None, None),
        ),
        check_vma=False,
    )
```

```python
import functools
import math

import jax
import jax.numpy as jnp
from jax import lax
from jax.experimental import pallas as pl
from jax.experimental.pallas import tpu as pltpu
from jax.sharding import PartitionSpec as P

QUERY_HEADS = 32
KEY_VALUE_HEADS = 4
HEAD_SIZE = 128
GROUP = QUERY_HEADS // KEY_VALUE_HEADS
HALF = KEY_VALUE_HEADS * HEAD_SIZE
PAIR = 2
SCALING = 1.0 / math.sqrt(HEAD_SIZE)

MASK_FILL = -1e30


def heads_to_rows(block, first, count):
    parts = [block[:, (first + i) * HEAD_SIZE : (first + i + 1) * HEAD_SIZE] for i in range(count)]
    return jnp.concatenate(parts, axis=0)


def head_gradients(query, cotangent, keys, values, bias, prob_ref, grad_ref, dq_ref):
    exponent = SCALING * math.log2(math.e)
    rows = query.shape[0]
    for pair in range(GROUP // PAIR):
        q = heads_to_rows(query, pair * PAIR, PAIR)
        c = heads_to_rows(cotangent, pair * PAIR, PAIR)
        scores = lax.dot_general(
            keys, q, (((1,), (1,)), ((), ())), preferred_element_type=jnp.float32
        )
        scores = bias(scores)
        prob_grad = lax.dot_general(
            values, c, (((1,), (1,)), ((), ())), preferred_element_type=jnp.float32
        )
        row_max = jnp.max(scores, axis=0, keepdims=True)
        weights = jnp.exp2((scores - row_max) * exponent)
        inverse = 1.0 / jnp.sum(weights, axis=0, keepdims=True)
        delta = jnp.sum(weights * prob_grad, axis=0, keepdims=True) * inverse
        probability = weights * inverse
        score_grad = (probability * (prob_grad - delta)).astype(jnp.bfloat16)
        columns = slice(pair * PAIR * rows, (pair + 1) * PAIR * rows)
        prob_ref[:, columns] = probability.astype(jnp.bfloat16)
        grad_ref[:, columns] = score_grad
        dq = lax.dot_general(
            score_grad, keys, (((0,), (0,)), ((), ())), preferred_element_type=jnp.float32
        )
        dq = (dq * SCALING).astype(jnp.bfloat16)
        for i in range(PAIR):
            at = (pair * PAIR + i) * HEAD_SIZE
            dq_ref[:, at : at + HEAD_SIZE] = dq[i * rows : (i + 1) * rows]
    key_grad = jnp.dot(
        grad_ref[...], heads_to_rows(query, 0, GROUP), preferred_element_type=jnp.float32
    )
    value_grad = jnp.dot(
        prob_ref[...], heads_to_rows(cotangent, 0, GROUP), preferred_element_type=jnp.float32
    )
    return (key_grad * SCALING).astype(jnp.bfloat16), value_grad.astype(jnp.bfloat16)


def remote(source, target, send, receive, ctx, comp):
    return pltpu.make_async_remote_copy(
        src_ref=source,
        dst_ref=target,
        send_sem=send,
        recv_sem=receive,
        device_id=(ctx, comp),
        device_id_type=pl.DeviceIdType.MESH,
    )


def greet(devices):
    barrier = pltpu.get_barrier_semaphore()
    for device in devices:
        pl.semaphore_signal(
            barrier, inc=1, device_id=device, device_id_type=pl.DeviceIdType.MESH
        )
    pl.semaphore_wait(barrier, len(devices))


def lanes_of(head):
    return [
        pl.ds(pl.multiple_of((head + shift) * HEAD_SIZE, HEAD_SIZE), HEAD_SIZE)
        for shift in (0, KEY_VALUE_HEADS)
    ]


def prompt_kernel(
    ctx_count, comp_count, q_ref, c_ref, kv_ref, dq_ref, own_ref, all_ref,
    whole, bias_ref, prob_ref, grad_ref, terms, pair_in, chip_terms, chip_in,
    up_send, up_recv, down_send, down_recv, pair_send, pair_recv,
    side_send, side_recv, pass_send, pass_recv, keep_sem,
    half_send, half_recv, term_send, term_recv,
):
    step = pl.program_id(0)
    place = lax.axis_index("ctx")
    column = lax.axis_index("comp")
    rows = q_ref.shape[0]
    total = ctx_count * rows
    chips = ctx_count // 2
    chip, core = place // 2, place % 2
    sibling = chip * 2 + 1 - core

    def other(offset):
        return (column + offset) % comp_count

    def up(t):
        at = (chip - t) * 2 + core
        return remote(whole.at[at], whole.at[at], up_send.at[t], up_recv.at[t], place + 2, column)

    def up_arrival(t):
        at = (chip - 1 - t) * 2 + core
        return remote(whole.at[at], whole.at[at], up_send.at[t], up_recv.at[t], place - 2, column)

    def down(t):
        at = (chip + t) * 2 + core
        return remote(
            whole.at[at], whole.at[at], down_send.at[t], down_recv.at[t], place - 2, column
        )

    def down_arrival(t):
        at = (chip + 1 + t) * 2 + core
        return remote(
            whole.at[at], whole.at[at], down_send.at[t], down_recv.at[t], place + 2, column
        )

    def to_sibling(k, side):
        at = k * 2 + side
        return remote(
            whole.at[at], whole.at[at], pair_send.at[k], pair_recv.at[k], sibling, column
        )

    def to_column(k, e):
        at = k * 2 + core
        return remote(
            whole.at[at],
            all_ref.at[column, at],
            side_send.at[e - 1, k],
            side_recv.at[e - 1, k],
            place,
            other(e),
        )

    def from_column(k, e):
        at = k * 2 + core
        source = other(comp_count - e)
        return remote(
            whole.at[at],
            all_ref.at[source, at],
            side_send.at[e - 1, k],
            side_recv.at[e - 1, k],
            place,
            source,
        )

    def pass_on(k, e, side):
        at = k * 2 + side
        source = other(comp_count - e)
        return remote(
            all_ref.at[source, at],
            all_ref.at[source, at],
            pass_send.at[e - 1, k],
            pass_recv.at[e - 1, k],
            sibling,
            column,
        )

    def half_over(h):
        return remote(
            terms.at[h, 1 - core], pair_in.at[h], half_send.at[h], half_recv.at[h], sibling, column
        )

    def terms_to(h, d):
        target = (chip + d) % chips
        return remote(
            chip_terms.at[h, target], chip_in.at[h, d - 1], term_send.at[h, d - 1],
            term_recv.at[h, d - 1], target * 2 + core, column,
        )

    def send_chip_terms(h):
        half_over(h).wait_recv()
        summed = terms[h, core].astype(jnp.float32) + pair_in[h].astype(jnp.float32)
        chip_terms[h] = summed.astype(jnp.bfloat16)
        for d in range(1, chips):
            terms_to(h, d).start()

    keep = pltpu.make_async_copy(whole, all_ref.at[column], keep_sem)

    def share(k):
        to_sibling(k, core).start()
        for e in range(1, comp_count):
            to_column(k, e).start()

    @pl.when(step == 0)
    def _():
        whole[place] = kv_ref[...]
        greetings = [(sibling, column)]
        greetings += [(place, other(e)) for e in range(1, comp_count)]
        greet(
            greetings + [((place + 2 * d) % ctx_count, column) for d in range(1, chips)]
        )
        for t in range(chips - 1):

            @pl.when((chip - t >= 0) & (chip + 1 < chips))
            def _():
                up(t).start()

            @pl.when((chip + t < chips) & (chip >= 1))
            def _():
                down(t).start()

            if t == 0:
                share(chip)

            @pl.when(chip - 1 - t >= 0)
            def _():
                up_arrival(t).wait_recv()
                share(chip - 1 - t)

            @pl.when(chip + 1 + t < chips)
            def _():
                down_arrival(t).wait_recv()
                share(chip + 1 + t)

        for k in range(chips):
            to_sibling(k, 1 - core).wait_recv()
        keep.start()
        shape = (total, rows)
        key_at = lax.broadcasted_iota(jnp.int32, shape, 0)
        row_at = lax.broadcasted_iota(jnp.int32, shape, 1)
        bias_ref[...] = jnp.where(key_at <= row_at + place * rows, 0.0, MASK_FILL)

    def bias(scores):
        return scores + jnp.concatenate([bias_ref[...]] * PAIR, axis=1)

    def head_of(shift):
        at = pl.multiple_of((step + shift) * HEAD_SIZE, HEAD_SIZE)
        return whole[:, :, pl.ds(at, HEAD_SIZE)].reshape(total, HEAD_SIZE)

    dk, dv = head_gradients(
        q_ref[...], c_ref[...], head_of(0), head_of(KEY_VALUE_HEADS), bias,
        prob_ref, grad_ref, dq_ref,
    )
    dk = dk.reshape(chips, 2, rows, HEAD_SIZE)
    dv = dv.reshape(chips, 2, rows, HEAD_SIZE)
    for side in range(2):
        terms[step, side, :, :, :HEAD_SIZE] = dk[:, side]
        terms[step, side, :, :, HEAD_SIZE:] = dv[:, side]
    half_over(step).start()

    @pl.when(step >= 1)
    def _():
        send_chip_terms(step - 1)

    for r in range(chips):

        @pl.when(step == min(r % KEY_VALUE_HEADS + 1, KEY_VALUE_HEADS - 1))
        def _():
            k = (chip + r) % chips
            for e in range(1, comp_count):
                from_column(k, e).wait_recv()
                pass_on(k, e, core).start()

    @pl.when(step == KEY_VALUE_HEADS - 1)
    def _():
        send_chip_terms(KEY_VALUE_HEADS - 1)
        for h in range(KEY_VALUE_HEADS):
            half_over(h).wait_send()
            summed = chip_terms[h, chip].astype(jnp.float32)
            for d in range(1, chips):
                terms_to(h, d).wait_recv()
                summed += chip_in[h, d - 1].astype(jnp.float32)
            own_ref[:, h * HEAD_SIZE : (h + 1) * HEAD_SIZE] = summed[:, :HEAD_SIZE]
            own_ref[:, HALF + h * HEAD_SIZE : HALF + (h + 1) * HEAD_SIZE] = summed[:, HEAD_SIZE:]
            for d in range(1, chips):
                terms_to(h, d).wait_send()

        for t in range(chips - 1):

            @pl.when((chip - t >= 0) & (chip + 1 < chips))
            def _():
                up(t).wait_send()

            @pl.when((chip + t < chips) & (chip >= 1))
            def _():
                down(t).wait_send()

        for k in range(chips):
            to_sibling(k, core).wait_send()
            for e in range(1, comp_count):
                to_column(k, e).wait_send()
                pass_on(k, e, core).wait_send()
                pass_on(k, e, 1 - core).wait_recv()
        keep.wait()


def completion_kernel(
    ctx_count, comp_count, length_ref, chooser_ref, q_ref, c_ref, k_ref, v_ref, own_k_ref, own_v_ref,
    prompt_ref, dq_ref, own_ref, out_ref,
    sum_ref, prob_ref, grad_ref, terms, arrived, table, table_in,
    send, recv, side_send, side_recv,
):
    step = pl.program_id(0)
    place = lax.axis_index("ctx")
    column = lax.axis_index("comp")
    rows = q_ref.shape[0]
    total = k_ref.shape[0]
    part = total // ctx_count
    length = length_ref[0]

    def other(offset):
        return (column + offset) % comp_count

    def out_to(h, d):
        target = (place + d) % ctx_count
        return remote(
            terms.at[h, target], arrived.at[h, d - 1], send.at[h, d - 1], recv.at[h, d - 1],
            target, column,
        )

    def across(h, e):
        return remote(
            table.at[h, e - 1], table_in.at[h, e - 1], side_send.at[h, e - 1],
            side_recv.at[h, e - 1], place, other(e),
        )

    @pl.when(step == 0)
    def _():
        greet(
            [((place + d) % ctx_count, column) for d in range(1, ctx_count)]
            + [(place, other(e)) for e in range(1, comp_count)]
        )

    key_at = lax.broadcasted_iota(jnp.int32, (rows, rows), 0)
    row_at = lax.broadcasted_iota(jnp.int32, (rows, rows), 1)
    own_bias = jnp.where((key_at <= row_at) & (key_at < length), 0.0, MASK_FILL)

    def bias(scores):
        own = scores[total:] + jnp.concatenate([own_bias] * PAIR, axis=1)
        return jnp.concatenate([scores[:total], own], axis=0)

    cotangent = c_ref[...]
    live = lax.broadcasted_iota(jnp.int32, cotangent.shape, 0) < length
    cotangent = jnp.where(live, cotangent, jnp.zeros_like(cotangent))
    keys = jnp.concatenate([k_ref[...], own_k_ref[...]], axis=0)
    values = jnp.concatenate([v_ref[...], own_v_ref[...]], axis=0)
    dk, dv = head_gradients(q_ref[...], cotangent, keys, values, bias, prob_ref, grad_ref, dq_ref)
    terms[step, :, :, :HEAD_SIZE] = dk[:total].reshape(ctx_count, part, HEAD_SIZE)
    terms[step, :, :, HEAD_SIZE:] = dv[:total].reshape(ctx_count, part, HEAD_SIZE)
    for d in range(1, ctx_count):
        out_to(step, d).start()
    key_lanes, value_lanes = lanes_of(step)
    own_ref[:, key_lanes] = dk[total:]
    own_ref[:, value_lanes] = dv[total:]

    @pl.when(step == KEY_VALUE_HEADS - 1)
    def _():
        def reduce_head(h, carry):
            for d in range(1, ctx_count):
                out_to(h, d).wait_recv()
            for e in list(range(1, comp_count)) + [0]:
                summed = terms[h, place].astype(jnp.float32) * chooser_ref[place, other(e)]
                for d in range(1, ctx_count):
                    source = (place + ctx_count - d) % ctx_count
                    weight = chooser_ref[source, other(e)]
                    summed += arrived[h, d - 1].astype(jnp.float32) * weight
                if e:
                    table[h, e - 1] = summed.astype(jnp.bfloat16)
                    across(h, e).start()
                else:
                    sum_ref[h] = summed
            return carry

        def finish_head(h, carry):
            summed = sum_ref[h]
            for e in range(1, comp_count):
                across(h, e).wait_recv()
                summed += table_in[h, e - 1].astype(jnp.float32)
            for at, lanes in enumerate(lanes_of(h)):
                part_sum = summed[:, at * HEAD_SIZE : (at + 1) * HEAD_SIZE]
                out_ref[:, lanes] = (part_sum + prompt_ref[:, lanes]).astype(jnp.bfloat16)
            for e in range(1, comp_count):
                across(h, e).wait_send()
            for d in range(1, ctx_count):
                out_to(h, d).wait_send()
            return carry

        lax.fori_loop(0, KEY_VALUE_HEADS, reduce_head, 0)
        lax.fori_loop(0, KEY_VALUE_HEADS, finish_head, 0)


def lane_block(rows, width, shift=0):
    return pl.BlockSpec((rows, width), lambda h: (0, h + shift))


def params(collective_id):
    return pltpu.CompilerParams(
        vmem_limit_bytes=56 * 1024 * 1024, collective_id=collective_id, has_side_effects=True
    )


def prompt_attention(query, cotangent, kv):
    ctx_count, comp_count = lax.axis_size("ctx"), lax.axis_size("comp")
    rows = query.shape[0]
    total = rows * ctx_count
    chips = ctx_count // 2
    wide = GROUP * HEAD_SIZE
    dma = pltpu.SemaphoreType.DMA
    return pl.pallas_call(
        functools.partial(prompt_kernel, ctx_count, comp_count),
        grid=(KEY_VALUE_HEADS,),
        in_specs=[
            lane_block(rows, wide),
            lane_block(rows, wide),
            pl.BlockSpec(kv.shape, lambda h: (0, 0)),
        ],
        out_specs=[
            lane_block(rows, wide),
            pl.BlockSpec(kv.shape, lambda h: (0, 0)),
            pl.BlockSpec(memory_space=pl.ANY),
        ],
        scratch_shapes=[
            pltpu.VMEM((ctx_count, rows, 2 * HALF), jnp.bfloat16),
            pltpu.VMEM((total, rows), jnp.float32),
            pltpu.VMEM((total, GROUP * rows), jnp.bfloat16),
            pltpu.VMEM((total, GROUP * rows), jnp.bfloat16),
            pltpu.VMEM((KEY_VALUE_HEADS, 2, chips, rows, 2 * HEAD_SIZE), jnp.bfloat16),
            pltpu.VMEM((KEY_VALUE_HEADS, chips, rows, 2 * HEAD_SIZE), jnp.bfloat16),
            pltpu.VMEM((KEY_VALUE_HEADS, chips, rows, 2 * HEAD_SIZE), jnp.bfloat16),
            pltpu.VMEM((KEY_VALUE_HEADS, chips - 1, rows, 2 * HEAD_SIZE), jnp.bfloat16),
        ]
        + [dma((chips - 1,))] * 4
        + [dma((chips,))] * 2
        + [dma((comp_count - 1, chips))] * 4
        + [dma]
        + [dma((KEY_VALUE_HEADS,))] * 2
        + [dma((KEY_VALUE_HEADS, chips - 1))] * 2,
        out_shape=[
            jax.ShapeDtypeStruct(query.shape, jnp.bfloat16),
            jax.ShapeDtypeStruct(kv.shape, jnp.float32),
            jax.ShapeDtypeStruct((comp_count, ctx_count, rows, 2 * HALF), jnp.bfloat16),
        ],
        compiler_params=params(1),
        name="prompt_attention",
    )(query, cotangent, kv)


def completion_attention(query, cotangent, kv, own_kv, prompt_sum, length, chooser):
    ctx_count, comp_count = lax.axis_size("ctx"), lax.axis_size("comp")
    rows, total = query.shape[0], kv.shape[0]
    part = total // ctx_count
    wide = GROUP * HEAD_SIZE
    dma = pltpu.SemaphoreType.DMA
    sums = (KEY_VALUE_HEADS, part, 2 * HEAD_SIZE)
    return pl.pallas_call(
        functools.partial(completion_kernel, ctx_count, comp_count),
        grid=(KEY_VALUE_HEADS,),
        in_specs=[
            pl.BlockSpec(memory_space=pltpu.SMEM),
            pl.BlockSpec(memory_space=pltpu.SMEM),
            lane_block(rows, wide),
            lane_block(rows, wide),
            lane_block(total, HEAD_SIZE),
            lane_block(total, HEAD_SIZE, KEY_VALUE_HEADS),
            lane_block(rows, HEAD_SIZE),
            lane_block(rows, HEAD_SIZE, KEY_VALUE_HEADS),
            pl.BlockSpec(prompt_sum.shape, lambda h: (0, 0)),
        ],
        out_specs=[
            lane_block(rows, wide),
            pl.BlockSpec(own_kv.shape, lambda h: (0, 0)),
            pl.BlockSpec(prompt_sum.shape, lambda h: (0, 0)),
        ],
        scratch_shapes=[
            pltpu.VMEM(sums, jnp.float32),
            pltpu.VMEM((total + rows, GROUP * rows), jnp.bfloat16),
            pltpu.VMEM((total + rows, GROUP * rows), jnp.bfloat16),
            pltpu.VMEM((KEY_VALUE_HEADS, ctx_count, part, 2 * HEAD_SIZE), jnp.bfloat16),
            pltpu.VMEM((KEY_VALUE_HEADS, ctx_count - 1, part, 2 * HEAD_SIZE), jnp.bfloat16),
            pltpu.VMEM((KEY_VALUE_HEADS, comp_count - 1, part, 2 * HEAD_SIZE), jnp.bfloat16),
            pltpu.VMEM((KEY_VALUE_HEADS, comp_count - 1, part, 2 * HEAD_SIZE), jnp.bfloat16),
            dma((KEY_VALUE_HEADS, ctx_count - 1)),
            dma((KEY_VALUE_HEADS, ctx_count - 1)),
            dma((KEY_VALUE_HEADS, comp_count - 1)),
            dma((KEY_VALUE_HEADS, comp_count - 1)),
        ],
        out_shape=[
            jax.ShapeDtypeStruct(query.shape, jnp.bfloat16),
            jax.ShapeDtypeStruct(own_kv.shape, jnp.bfloat16),
            jax.ShapeDtypeStruct(prompt_sum.shape, jnp.bfloat16),
        ],
        compiler_params=params(2),
        name="completion_attention",
    )(length, chooser, query, cotangent, kv, kv, own_kv, own_kv, prompt_sum)


def local(prompt_query, prompt_kv, prompt_cot, comp_query, comp_kv, comp_cot, group_of, lengths):
    ctx_count = lax.axis_size("ctx")
    comp_count = lax.axis_size("comp")
    ctx_place = lax.axis_index("ctx")
    comp_place = lax.axis_index("comp")
    column_groups = jnp.take(group_of.reshape(ctx_count, comp_count), comp_place, axis=1)
    chooser = column_groups[:, None] == jnp.arange(comp_count, dtype=jnp.int32)[None, :]
    length = lax.dynamic_slice_in_dim(lengths, ctx_place * comp_count + comp_place, 1)
    prompt_dq, prompt_sum, prompts = prompt_attention(
        prompt_query[0], prompt_cot[0], prompt_kv[0]
    )
    group_prompt = lax.dynamic_index_in_dim(prompts, column_groups[ctx_place], 0, keepdims=False)
    comp_dq, own_dkv, summed = completion_attention(
        comp_query[0],
        comp_cot[0],
        group_prompt.reshape(-1, 2 * HALF),
        comp_kv[0],
        prompt_sum,
        length,
        chooser.astype(jnp.float32),
    )
    return prompt_dq[None], summed[None], comp_dq[None], own_dkv[None]


def solution(mesh):
    placed = (
        P("comp", "ctx", None),
        P("comp", "ctx", None),
        P("comp", "ctx", None),
        P(("ctx", "comp"), None, None),
        P(("ctx", "comp"), None, None),
        P(("ctx", "comp"), None, None),
        P(),
        P(),
    )
    return jax.shard_map(
        local,
        mesh=mesh,
        in_specs=placed,
        out_specs=(
            P("comp", "ctx", None),
            P("comp", "ctx", None),
            P(("ctx", "comp"), None, None),
            P(("ctx", "comp"), None, None),
        ),
        check_vma=False,
    )
```
